768 devices in a mesh: ein: 32 (over y, x_lo, core), eout: 24 (over z, x_hi).
Axes of the slice: x: 4 (x_hi: 2, x_lo: 2; x = x_hi * 2 + x_lo), y: 8, z: 12, core: 2. Of those that a mesh axis runs over, the one named last changes fastest.
Arguments:
- activations: bfloat16 [768, 28672], P('eout', 'ein'), may hold values from -6 to 6
- gradients: bfloat16 [768, 8192], P('eout'), may hold values from -6 to 6
- eigvec_in: bfloat16 [28672, 24576], P('ein', 'eout'), may hold values from -0.03125 to 0.03125
- eigvec_out: bfloat16 [8192, 8192], P(None, 'ein'), may hold values from -0.0625 to 0.0625
- lengths: int32 [2], replicated, may hold values from 96 to 384
Outputs:
- correction: float32 [24576, 8192], P('eout', 'ein')
The draws below stay inside these ranges and needn't reach their ends.
All inputs are finite; a program needn't handle non-finite values.
Results may differ from the reference program's by a relative error of at most 0.0044.
Values may be sent and summed in bfloat16 or wider, within the bound.
A program may use at most 32 MiB of HBM per device.

```python
import jax
import jax.numpy as jnp
from jax import lax

DIN = 28672
DOUT = 8192
LEN = 384
DOCS = 2
KA = 24576
KG = 8192
TOKENS = 768


def steps_of(key, shape, split, smallest, high):
    factor_of = 1.0
    for axis_at, shards_of in split:
        draws = jax.random.uniform(jax.random.fold_in(jax.random.fold_in(key, 6), axis_at), (shards_of,), jnp.float32, smallest / len(split), high / len(split))
        factor_of = factor_of * jnp.repeat(jnp.exp(draws), shape[axis_at] // shards_of).reshape((-1,) + (1,) * (len(shape) - 1 - axis_at))
    return factor_of


def normal_values(rng, shape, deviation, reach, cuts=(), kind=jnp.bfloat16):
    result = deviation * jax.random.normal(rng, shape, jnp.float32)
    if cuts:
        result = result * steps_of(rng, shape, cuts, -0.22, 0.18)
    return jnp.clip(result, -reach, reach).astype(kind)


def setup_inputs(seed: int = 0) -> dict:
    seeds = jax.random.split(jax.random.key(seed), 6)
    return {
        "activations": normal_values(seeds[0], (TOKENS, DIN), 1.0, 6.0, ((0, 24), (1, 32))),
        "gradients": normal_values(seeds[1], (TOKENS, DOUT), 1.0, 6.0, ((0, 24),)),
        "eigvec_in": normal_values(seeds[2], (DIN, KA), DIN ** -0.5, 0.03125, ((0, 32), (1, 24))),
        "eigvec_out": normal_values(seeds[3], (DOUT, KG), DOUT ** -0.5, 0.0625, ((1, 32),)),
        "lengths": jax.random.randint(seeds[4], (DOCS,), LEN // 4, LEN + 1).astype(jnp.int32),
    }


def reference(activations, gradients, eigvec_in, eigvec_out, lengths):
    rotated_act = jnp.dot(activations, eigvec_in, preferred_element_type=jnp.float32).astype(jnp.bfloat16)
    positions = jnp.arange(DOCS * LEN, dtype=jnp.int32)
    limits = jnp.repeat(lengths, LEN)
    kept = (positions % LEN) < limits
    grad_full = jnp.dot(gradients, eigvec_out, preferred_element_type=jnp.float32)
    rotated_grad = jnp.where(kept[:, None], grad_full, jnp.zeros_like(grad_full)).astype(jnp.bfloat16)
    act_docs = rotated_act.reshape(DOCS, LEN, KA)
    grad_docs = rotated_grad.reshape(DOCS, LEN, KG)

    def accumulate(running, blocks):
        rotated_doc = jnp.dot(blocks[0].T, blocks[1], preferred_element_type=jnp.float32)
        return running + rotated_doc * rotated_doc, None

    squares, _ = lax.scan(accumulate, jnp.zeros((KA, KG), jnp.float32), (act_docs, grad_docs))
    return squares / jnp.sum(lengths).astype(jnp.float32)
```

```python
import jax
import jax.numpy as jnp
from jax import lax
from jax.experimental import pallas as pl
from jax.experimental.pallas import tpu as pltpu
from jax.sharding import PartitionSpec as P

LEN = 384
MESH = pl.DeviceIdType.MESH
F32 = jnp.float32
BF16 = jnp.bfloat16

NZ = 12
NY = 8
SIZES = (192, 256, 256, 64)
OFFS = (0, 192, 448, 704)
SLOT = 64
HALF = 32


def up(k):
    return 0 if k == 0 else 2 * k - 1


def down(k):
    return 2 * k if k < 6 else 11


def kernel(
    act_in, grad_in, wi_in, wo_in, lengths, out,
    act, grads, wi, wo, gall, gdoc, part, core_r, x_s, x_r, y_s, y_r, full,
    local_sem, z_ss, z_rs, g_ss, g_rs, r_ss, r_rs,
):
    ein = lax.axis_index("ein")
    eout = lax.axis_index("eout")
    core = lax.rem(ein, 2)
    x_lo = lax.rem(lax.div(ein, 2), 2)
    y = lax.div(ein, 4)
    x_hi = lax.rem(eout, 2)
    z = lax.div(eout, 2)

    z_up = (ein, lax.rem(z + 1, NZ) * 2 + x_hi)
    z_dn = (ein, lax.rem(z + NZ - 1, NZ) * 2 + x_hi)
    hi_peer = (ein, z * 2 + 1 - x_hi)
    core_peer = (ein + 1 - 2 * core, eout)
    x_peer = (ein + 2 - 4 * x_lo, eout)
    y_of = [lax.rem(y + d, NY) for d in range(NY)]
    y_peer = [(y_of[d] * 4 + x_lo * 2 + core, eout) for d in range(NY)]

    act_copy = pltpu.make_async_copy(act_in, act.at[pl.ds(0, HALF)], local_sem.at[0])
    act_copy.start()
    grad_copy = pltpu.make_async_copy(grad_in, grads, local_sem.at[1])
    grad_copy.start()
    wo_copies = []
    for i in range(4):
        rows = pl.ds(i * 2048, 2048)
        wo_copies.append(pltpu.make_async_copy(wo_in.at[rows], wo.at[rows], local_sem.at[2 + i]))
        wo_copies[-1].start()
    wi_copy = pltpu.make_async_copy(wi_in, wi, local_sem.at[6])
    wi_copy.start()

    barrier = pltpu.get_barrier_semaphore()
    partners = [z_up, z_dn, hi_peer, core_peer, x_peer] + y_peer[1:]
    for peer in partners:
        pl.semaphore_signal(barrier, inc=1, device_id=peer, device_id_type=MESH)
    pl.semaphore_wait(barrier, len(partners))

    started = []

    def send(src, dst, ss, rs, peer):
        copy = pltpu.make_async_remote_copy(
            src_ref=src, dst_ref=dst, send_sem=ss, recv_sem=rs,
            device_id=peer, device_id_type=MESH,
        )
        copy.start()
        started.append(copy)
        return copy

    z_in = {}

    def act_unit(slot, h):
        return act.at[pl.ds(slot * SLOT + h * HALF, HALF)]

    def z_send(k, h):
        if k < 6 and not (k == 5 and h == 1):
            i = (k * 2 + h) * 2
            z_in["u", k + 1, h] = send(
                act_unit(up(k), h), act_unit(up(k + 1) if k < 5 else 11, h),
                z_ss.at[i], z_rs.at[i], z_dn)
        if k < 6 and not (k == 5 and h == 0):
            i = (k * 2 + h) * 2 + 1
            z_in["d", k + 1, h] = send(
                act_unit(down(k), h), act_unit(down(k + 1), h),
                z_ss.at[i], z_rs.at[i], z_up)

    def z_serve(k, h):
        if k == 0:
            hi_act.wait_recv()
            z_send(0, 1)
            return
        for way in "ud":
            if (way, k, h) in z_in:
                z_in[way, k, h].wait_recv()
        if k < 6:
            z_send(k, h)

    g_in = {}

    def g_rows(slot, h=None):
        if h is None:
            return gall.at[pl.ds(slot * SLOT, SLOT)]
        return gall.at[pl.ds(slot * SLOT + h * HALF, HALF)]

    def g_serve(k):
        if k == 0:
            hi_grad.wait_recv()
        else:
            for way in "ud":
                g_in[way, k].wait_recv()
        if k < 5:
            g_in["u", k + 1] = send(g_rows(up(k)), g_rows(up(k + 1)), g_ss.at[2 * k], g_rs.at[2 * k], z_dn)
            g_in["d", k + 1] = send(g_rows(down(k)), g_rows(down(k + 1)), g_ss.at[2 * k + 1], g_rs.at[2 * k + 1], z_up)
        elif k == 5:
            g_in["u", 6] = send(g_rows(up(5), 0), g_rows(11, 0), g_ss.at[10], g_rs.at[10], z_dn)
            g_in["d", 6] = send(g_rows(down(5), 1), g_rows(11, 1), g_ss.at[11], g_rs.at[11], z_up)

    def grad_part(first, count, total):
        def step(i, acc):
            at = pl.multiple_of(i * 1024, 1024)
            return acc + jnp.dot(
                grads[:, pl.ds(at, 1024)], wo[pl.ds(at, 1024), :], preferred_element_type=F32)
        return lax.fori_loop(first, first + count, step, total)

    def grad_done(total):
        limit = jnp.where(z < NZ // 2, lengths[0], lengths[1])
        start = lax.rem(z, NZ // 2) * SLOT + x_hi * HALF
        position = start + lax.broadcasted_iota(jnp.int32, (HALF, 256), 0)
        gall[pl.ds(0, HALF), :] = jnp.where(position < limit, total, 0.0).astype(BF16)

    red = {}

    def off2(g):
        return OFFS[g] // 2

    def off4(g):
        return OFFS[g] // 4

    def quarter(g, c, x):
        n = SIZES[g] // 4
        return pl.ds(pl.multiple_of(OFFS[g] + (c * 2 + x) * n, 16), n)

    def sem(g, i):
        return r_ss.at[g * 19 + i], r_rs.at[g * 19 + i]

    def gemm(g):
        rows = pl.ds(OFFS[g], SIZES[g])

        def step(c, carry):
            cols = pl.ds(pl.multiple_of(c * 256, 256), 256)
            product = jnp.dot(act[rows, :], wi[:, cols], preferred_element_type=F32)
            part[2 * c, rows, :] = product[:, :128]
            part[2 * c + 1, rows, :] = product[:, 128:]
            return carry

        lax.fori_loop(0, 4, step, 0)
        n = SIZES[g] // 2
        theirs = pl.ds(pl.multiple_of(OFFS[g] + (1 - core) * n, 16), n)
        red["c", g] = send(part.at[:, theirs], core_r.at[:, pl.ds(off2(g), n)], *sem(g, 0), core_peer)

    def in_half(g, x):
        n = SIZES[g] // 4
        return pl.ds(pl.multiple_of(off2(g) + x * n, 16), n)

    def stage_c(g):
        red["c", g].wait_recv()
        n = SIZES[g] // 4
        mine, got = quarter(g, core, 1 - x_lo), in_half(g, 1 - x_lo)

        def step(b, carry):
            x_s[b, pl.ds(off4(g), n), :] = (part[b, mine, :] + core_r[b, got, :]).astype(BF16)
            return carry

        lax.fori_loop(0, NY, step, 0)
        rows = pl.ds(off4(g), n)
        red["x", g] = send(x_s.at[:, rows], x_r.at[:, rows], *sem(g, 1), x_peer)

    def chip_pair_sum(g, b):
        n = SIZES[g] // 4
        return (part[b, quarter(g, core, x_lo), :] + core_r[b, in_half(g, x_lo), :]
                + x_r[b, pl.ds(off4(g), n), :].astype(F32))

    def stage_x(g):
        red["x", g].wait_recv()
        n = SIZES[g] // 4
        rows = pl.ds(off4(g), n)

        def step(b, carry):
            y_s[b, rows, :] = chip_pair_sum(g, b).astype(BF16)
            return carry

        lax.fori_loop(0, NY, step, 0)
        for d in (4, 3, 5, 2, 6, 1, 7):
            red["y", g, d] = send(
                y_s.at[y_of[d], rows], y_r.at[d - 1, rows], *sem(g, 1 + d), y_peer[d])

    def stage_y(g):
        n = SIZES[g] // 4
        rows = pl.ds(off4(g), n)
        total = chip_pair_sum(g, y)
        for d in range(1, NY):
            red["y", g, d].wait_recv()
        for d in range(1, NY):
            total = total + y_r[d - 1, rows, :].astype(F32)
        mine = quarter(g, core, x_lo)
        full[y, mine, :] = total.astype(BF16)
        for d in (4, 3, 5, 2, 6, 1, 7):
            red["f", g, d] = send(
                full.at[y, mine], full.at[y, mine], *sem(g, 8 + d), y_peer[d])

    def stage_f(g):
        mine = quarter(g, core, x_lo)
        for d in range(1, NY):
            recv = pltpu.make_async_remote_copy(
                src_ref=full.at[y, mine], dst_ref=full.at[y_of[NY - d], mine],
                send_sem=sem(g, 8 + d)[0], recv_sem=sem(g, 8 + d)[1],
                device_id=y_peer[d], device_id_type=MESH)
            recv.wait_recv()
        red["fx", g] = send(full.at[:, mine], full.at[:, mine], *sem(g, 16), x_peer)
        red["fc", g] = send(full.at[:, mine], full.at[:, mine], *sem(g, 17), core_peer)

    def wait_at(g, i, c, x, peer):
        rows = quarter(g, c, x)
        pltpu.make_async_remote_copy(
            src_ref=full.at[:, rows], dst_ref=full.at[:, rows],
            send_sem=sem(g, i)[0], recv_sem=sem(g, i)[1],
            device_id=peer, device_id_type=MESH).wait_recv()

    def stage_fx(g):
        wait_at(g, 16, core, 1 - x_lo, x_peer)
        theirs = quarter(g, core, 1 - x_lo)
        red["fxc", g] = send(full.at[:, theirs], full.at[:, theirs], *sem(g, 18), core_peer)

    def stage_fc(g):
        wait_at(g, 17, 1 - core, x_lo, core_peer)
        wait_at(g, 18, 1 - core, 1 - x_lo, core_peer)

    act_copy.wait()
    z_send(0, 0)
    hi_act = send(act_unit(0, 0), act_unit(0, 1), z_ss.at[24], z_rs.at[24], hi_peer)
    grad_copy.wait()
    for copy in wo_copies[:2]:
        copy.wait()
    total = grad_part(0, 4, jnp.zeros((HALF, 256), F32))
    z_serve(0, 1)
    for copy in wo_copies[2:]:
        copy.wait()
    grad_done(grad_part(4, 4, total))
    hi_grad = send(g_rows(0, 0), g_rows(0, 1), g_ss.at[12], g_rs.at[12], hi_peer)
    z_serve(1, 0)
    wi_copy.wait()
    z_serve(1, 1)
    gemm(0)
    z_serve(2, 0)
    g_serve(0)
    z_serve(2, 1)
    stage_c(0)
    z_serve(3, 0)
    g_serve(1)
    z_serve(3, 1)
    gemm(1)
    stage_x(0)
    z_serve(4, 0)
    stage_c(1)
    g_serve(2)
    z_serve(4, 1)
    stage_y(0)
    z_serve(5, 0)
    stage_x(1)
    g_serve(3)
    z_serve(5, 1)
    gemm(2)
    g_serve(4)
    stage_f(0)
    z_serve(6, 0)
    z_serve(6, 1)
    gemm(3)
    stage_c(2)
    stage_c(3)
    stage_y(1)
    stage_fx(0)
    g_serve(5)
    stage_x(2)
    stage_x(3)
    stage_f(1)
    g_serve(6)

    for slot in range(NZ):
        k = (slot + 1) // 2
        shift = k if slot % 2 else NZ - k
        doc = lax.div(lax.rem(z + shift, NZ), NZ // 2)
        rows = pl.ds(slot * SLOT, SLOT)
        values = gall[rows, :]
        zero = jnp.zeros_like(values)
        gdoc[rows, 0:256] = jnp.where(doc == 0, values, zero)
        gdoc[rows, 256:512] = jnp.where(doc == 1, values, zero)

    stage_fx(1)
    stage_y(2)
    stage_y(3)
    stage_f(2)
    stage_f(3)
    stage_fx(2)
    stage_fx(3)
    for g in range(4):
        stage_fc(g)

    denominator = (lengths[0] + lengths[1]).astype(F32)

    def outer(b, carry):
        both = lax.dot_general(
            full[b], gdoc[...], (((0,), (0,)), ((), ())), preferred_element_type=F32)
        squares = both[:, :256] * both[:, :256] + both[:, 256:] * both[:, 256:]
        out[pl.ds(pl.multiple_of(b * 128, 128), 128), :] = squares / denominator
        return carry

    lax.fori_loop(0, NY, outer, 0)

    for copy in started:
        copy.wait_send()


def body(activations, gradients, eigvec_in, eigvec_out, lengths):
    anywhere = pl.BlockSpec(memory_space=pl.ANY)
    dma = pltpu.SemaphoreType.DMA
    return pl.pallas_call(
        kernel,
        out_shape=jax.ShapeDtypeStruct((1024, 256), F32),
        in_specs=[anywhere] * 4 + [pl.BlockSpec(memory_space=pltpu.SMEM)],
        out_specs=pl.BlockSpec(memory_space=pltpu.VMEM),
        scratch_shapes=[
            pltpu.VMEM((768, 896), BF16),
            pltpu.VMEM((32, 8192), BF16),
            pltpu.VMEM((896, 1024), BF16),
            pltpu.VMEM((8192, 256), BF16),
            pltpu.VMEM((768, 256), BF16),
            pltpu.VMEM((768, 512), BF16),
            pltpu.VMEM((8, 768, 128), F32),
            pltpu.VMEM((8, 384, 128), F32),
            pltpu.VMEM((8, 192, 128), BF16),
            pltpu.VMEM((8, 192, 128), BF16),
            pltpu.VMEM((8, 192, 128), BF16),
            pltpu.VMEM((7, 192, 128), BF16),
            pltpu.VMEM((8, 768, 128), BF16),
            dma((7,)),
            dma((25,)),
            dma((25,)),
            dma((13,)),
            dma((13,)),
            dma((76,)),
            dma((76,)),
        ],
        compiler_params=pltpu.CompilerParams(
            collective_id=0, has_side_effects=True, vmem_limit_bytes=40 * 1024 * 1024),
        cost_estimate=pl.CostEstimate(
            flops=2_300_000_000, bytes_accessed=8_000_000, transcendentals=0),
    )(activations, gradients, eigvec_in, eigvec_out, lengths)


def solution(mesh):
    in_specs = (P("eout", "ein"), P("eout", None), P("ein", "eout"), P(None, "ein"), P())
    out_specs = P("eout", "ein")
    return jax.shard_map(body, mesh=mesh, in_specs=in_specs, out_specs=out_specs, check_vma=False)
```

```python
import jax
import jax.numpy as jnp
from jax import lax
from jax.experimental import pallas as pl
from jax.experimental.pallas import tpu as pltpu
from jax.sharding import PartitionSpec as P

LEN = 384
MESH = pl.DeviceIdType.MESH
F32 = jnp.float32
BF16 = jnp.bfloat16

NZ = 12
NY = 8
SIZES = (192, 128, 128, 128, 192)
OFFS = tuple(sum(SIZES[:g]) for g in range(len(SIZES)))
SLOT = 64
HALF = 32
SCHEDULE = [
    ("z0",), ("wi",), ("grad1",), ("z", 0, 1), ("z", 2, 0), ("grad2",), ("z", 2, 1), ("mm", 1),
    ("zw", 1), ("mm", 0), ("c", 1), ("c", 0), ("z", 4, 0), ("x", 1), ("z", 4, 1), ("zw", 3),
    ("mm", 2), ("mm", 3), ("x", 0), ("c", 2), ("c", 3), ("y", 1), ("g", 0), ("zw", 6), ("zw", 5),
    ("mm", 4), ("x", 2), ("c", 4), ("x", 3), ("y", 0), ("g", 2), ("f", 1), ("x", 4), ("y", 3),
    ("gw", 3), ("f", 0), ("gw", 1), ("y", 2), ("y", 4), ("fx", 1), ("g", 4), ("fx", 0), ("f", 3),
    ("f", 2), ("fx", 3), ("gw", 5), ("f", 4), ("gw", 6), ("fx", 2), ("docs",), ("fc", 3), ("fc", 0),
    ("fc", 1), ("fc", 2), ("outer", 0), ("fx", 4), ("fc", 4), ("outer", 1),
]


def up(k):
    return 0 if k == 0 else 2 * k - 1


def down(k):
    return 2 * k if k < 6 else 11


def kernel(
    act_in, grad_in, wi_in, wo_in, lengths, out,
    act, grads, wi, wo, gall, gdoc, part, core_r, x_s, x_r, y_s, y_r, full, prod,
    local_sem, z_ss, z_rs, g_ss, g_rs, r_ss, r_rs,
):
    ein = lax.axis_index("ein")
    eout = lax.axis_index("eout")
    core = lax.rem(ein, 2)
    x_lo = lax.rem(lax.div(ein, 2), 2)
    y = lax.div(ein, 4)
    x_hi = lax.rem(eout, 2)
    z = lax.div(eout, 2)

    z_peer = {
        ("u", n): (ein, lax.rem(z + NZ - n, NZ) * 2 + x_hi) for n in (1, 2)
    } | {("d", n): (ein, lax.rem(z + n, NZ) * 2 + x_hi) for n in (1, 2)}
    hi_peer = (ein, z * 2 + 1 - x_hi)
    core_peer = (ein + 1 - 2 * core, eout)
    x_peer = (ein + 2 - 4 * x_lo, eout)
    y_of = [lax.rem(y + d, NY) for d in range(NY)]
    y_peer = [(y_of[d] * 4 + x_lo * 2 + core, eout) for d in range(NY)]

    act_copy = pltpu.make_async_copy(act_in, act.at[pl.ds(0, HALF)], local_sem.at[0])
    act_copy.start()
    grad_copy = pltpu.make_async_copy(grad_in, grads, local_sem.at[1])
    grad_copy.start()
    wo_copies = []
    for i in range(4):
        rows = pl.ds(i * 2048, 2048)
        wo_copies.append(pltpu.make_async_copy(wo_in.at[rows], wo.at[rows], local_sem.at[2 + i]))
        wo_copies[-1].start()
    wi_copy = pltpu.make_async_copy(wi_in, wi, local_sem.at[6])
    wi_copy.start()

    barrier = pltpu.get_barrier_semaphore()
    partners = [*z_peer.values(), hi_peer, core_peer, x_peer, *y_peer[1:]]
    for peer in partners:
        pl.semaphore_signal(barrier, inc=1, device_id=peer, device_id_type=MESH)
    pl.semaphore_wait(barrier, len(partners))

    started = []
    state = {}

    def send(src, dst, ss, rs, peer):
        copy = pltpu.make_async_remote_copy(
            src_ref=src, dst_ref=dst, send_sem=ss, recv_sem=rs,
            device_id=peer, device_id_type=MESH,
        )
        copy.start()
        started.append(copy)
        return copy

    z_in = {}

    def act_unit(slot, h):
        return act.at[pl.ds(slot * SLOT + h * HALF, HALF)]

    slot_of = {"u": up, "d": down}

    def z_send(way, k, h, n):
        if k + n == 6 and way != "ud"[h]:
            return
        i = (k + n) * 4 + h * 2 + "ud".index(way)
        to = 11 if k + n == 6 else slot_of[way](k + n)
        z_in[way, k + n, h] = send(
            act_unit(slot_of[way](k), h), act_unit(to, h), z_ss.at[i], z_rs.at[i], z_peer[way, n])

    def z_serve(k, h):
        if k == 0 and h == 1:
            state["hi_act"].wait_recv()
        for way in "ud":
            if k > 0:
                z_in[way, k, h].wait_recv()
            z_send(way, k, h, 2)
            if k > 0:
                z_send(way, k, h, 1)
        if k == 0:
            for way in "ud":
                z_send(way, k, h, 1)

    def z_wait(k):
        for h in range(2):
            for way in "ud":
                if (way, k, h) in z_in:
                    z_in[way, k, h].wait_recv()

    g_in = {}

    def g_rows(slot, h=None):
        if h is None:
            return gall.at[pl.ds(slot * SLOT, SLOT)]
        return gall.at[pl.ds(slot * SLOT + h * HALF, HALF)]

    def g_send(way, k, n):
        i = (k + n) * 2 + "ud".index(way)
        h = "ud".index(way) if k + n == 6 else None
        to = 11 if k + n == 6 else slot_of[way](k + n)
        g_in[way, k + n] = send(
            g_rows(slot_of[way](k), h), g_rows(to, h), g_ss.at[i], g_rs.at[i], z_peer[way, n])

    def g_serve(k):
        if k == 0:
            state["hi"].wait_recv()
        for way in "ud":
            if k > 0:
                g_in[way, k].wait_recv()
            g_send(way, k, 2)
            g_send(way, k, 1)

    def g_wait(k):
        for way in "ud":
            g_in[way, k].wait_recv()

    def grad_part(first, count, total):
        def step(i, acc):
            at = pl.multiple_of(i * 1024, 1024)
            return acc + jnp.dot(
                grads[:, pl.ds(at, 1024)], wo[pl.ds(at, 1024), :], preferred_element_type=F32)
        return lax.fori_loop(first, first + count, step, total)

    def grad_done(total):
        limit = jnp.where(z < NZ // 2, lengths[0], lengths[1])
        start = lax.rem(z, NZ // 2) * SLOT + x_hi * HALF
        position = start + lax.broadcasted_iota(jnp.int32, (HALF, 256), 0)
        gall[pl.ds(0, HALF), :] = jnp.where(position < limit, total, 0.0).astype(BF16)

    red = {}

    def off2(g):
        return OFFS[g] // 2

    def off4(g):
        return OFFS[g] // 4

    def quarter(g, c, x):
        n = SIZES[g] // 4
        return pl.ds(pl.multiple_of(OFFS[g] + (c * 2 + x) * n, 16), n)

    def sem(g, i):
        return r_ss.at[g * 19 + i], r_rs.at[g * 19 + i]

    def gemm(g):
        rows = pl.ds(OFFS[g], SIZES[g])

        def step(c, carry):
            cols = pl.ds(pl.multiple_of(c * 256, 256), 256)
            product = jnp.dot(act[rows, :], wi[:, cols], preferred_element_type=F32)
            part[2 * c, rows, :] = product[:, :128]
            part[2 * c + 1, rows, :] = product[:, 128:]
            return carry

        lax.fori_loop(0, 4, step, 0)
        n = SIZES[g] // 2
        theirs = pl.ds(pl.multiple_of(OFFS[g] + (1 - core) * n, 16), n)
        red["c", g] = send(part.at[:, theirs], core_r.at[:, pl.ds(off2(g), n)], *sem(g, 0), core_peer)

    def in_half(g, x):
        n = SIZES[g] // 4
        return pl.ds(pl.multiple_of(off2(g) + x * n, 16), n)

    def stage_c(g):
        red["c", g].wait_recv()
        n = SIZES[g] // 4
        mine, got = quarter(g, core, 1 - x_lo), in_half(g, 1 - x_lo)

        def step(b, carry):
            x_s[b, pl.ds(off4(g), n), :] = (part[b, mine, :] + core_r[b, got, :]).astype(BF16)
            return carry

        lax.fori_loop(0, NY, step, 0)
        rows = pl.ds(off4(g), n)
        red["x", g] = send(x_s.at[:, rows], x_r.at[:, rows], *sem(g, 1), x_peer)

    def chip_pair_sum(g, b):
        n = SIZES[g] // 4
        return (part[b, quarter(g, core, x_lo), :] + core_r[b, in_half(g, x_lo), :]
                + x_r[b, pl.ds(off4(g), n), :].astype(F32))

    def stage_x(g):
        red["x", g].wait_recv()
        n = SIZES[g] // 4
        rows = pl.ds(off4(g), n)

        def step(b, carry):
            y_s[b, rows, :] = chip_pair_sum(g, b).astype(BF16)
            return carry

        lax.fori_loop(0, NY, step, 0)
        for d in (4, 3, 5, 2, 6, 1, 7):
            red["y", g, d] = send(
                y_s.at[y_of[d], rows], y_r.at[d - 1, rows], *sem(g, 1 + d), y_peer[d])

    def stage_y(g):
        n = SIZES[g] // 4
        rows = pl.ds(off4(g), n)
        total = chip_pair_sum(g, y)
        for d in range(1, NY):
            red["y", g, d].wait_recv()
        for d in range(1, NY):
            total = total + y_r[d - 1, rows, :].astype(F32)
        mine = quarter(g, core, x_lo)
        full[y, mine, :] = total.astype(BF16)
        for d in (4, 3, 5, 2, 6, 1, 7):
            red["f", g, d] = send(
                full.at[y, mine], full.at[y, mine], *sem(g, 8 + d), y_peer[d])

    def stage_f(g):
        mine = quarter(g, core, x_lo)
        for d in range(1, NY):
            recv = pltpu.make_async_remote_copy(
                src_ref=full.at[y, mine], dst_ref=full.at[y_of[NY - d], mine],
                send_sem=sem(g, 8 + d)[0], recv_sem=sem(g, 8 + d)[1],
                device_id=y_peer[d], device_id_type=MESH)
            recv.wait_recv()
        red["fx", g] = send(full.at[:, mine], full.at[:, mine], *sem(g, 16), x_peer)
        red["fc", g] = send(full.at[:, mine], full.at[:, mine], *sem(g, 17), core_peer)

    def wait_at(g, i, c, x, peer):
        rows = quarter(g, c, x)
        pltpu.make_async_remote_copy(
            src_ref=full.at[:, rows], dst_ref=full.at[:, rows],
            send_sem=sem(g, i)[0], recv_sem=sem(g, i)[1],
            device_id=peer, device_id_type=MESH).wait_recv()

    def stage_fx(g):
        wait_at(g, 16, core, 1 - x_lo, x_peer)
        theirs = quarter(g, core, 1 - x_lo)
        red["fxc", g] = send(full.at[:, theirs], full.at[:, theirs], *sem(g, 18), core_peer)

    def stage_fc(g):
        wait_at(g, 17, 1 - core, x_lo, core_peer)
        wait_at(g, 18, 1 - core, 1 - x_lo, core_peer)

    def grad_first():
        grad_copy.wait()
        for copy in wo_copies[:2]:
            copy.wait()
        state["total"] = grad_part(0, 4, jnp.zeros((HALF, 256), F32))

    def grad_last():
        for copy in wo_copies[2:]:
            copy.wait()
        grad_done(grad_part(4, 4, state["total"]))
        state["hi"] = send(g_rows(0, 0), g_rows(0, 1), g_ss.at[0], g_rs.at[0], hi_peer)

    def documents():
        for slot in range(NZ):
            k = (slot + 1) // 2
            shift = k if slot % 2 else NZ - k
            doc = lax.div(lax.rem(z + shift, NZ), NZ // 2)
            rows = pl.ds(slot * SLOT, SLOT)
            values = gall[rows, :]
            zero = jnp.zeros_like(values)
            gdoc[rows, 0:256] = jnp.where(doc == 0, values, zero)
            gdoc[rows, 256:512] = jnp.where(doc == 1, values, zero)

    def outer(last):
        rows = pl.ds(OFFS[-1], SIZES[-1]) if last else pl.ds(0, OFFS[-1])
        if last:
            denominator = (lengths[0] + lengths[1]).astype(F32)

        def step(b, carry):
            both = lax.dot_general(
                full[b, rows, :], gdoc[rows, :], (((0,), (0,)), ((), ())),
                preferred_element_type=F32)
            if last:
                both = both + prod[b]
                squares = both[:, :256] * both[:, :256] + both[:, 256:] * both[:, 256:]
                out[pl.ds(pl.multiple_of(b * 128, 128), 128), :] = squares / denominator
            else:
                prod[b] = both
            return carry

        lax.fori_loop(0, NY, step, 0)

    def z_first():
        state["hi_act"] = send(act_unit(0, 0), act_unit(0, 1), z_ss.at[0], z_rs.at[0], hi_peer)
        z_serve(0, 0)

    steps = {
        "z0": z_first, "z": z_serve, "wi": wi_copy.wait, "g": g_serve, "grad1": grad_first,
        "grad2": grad_last, "mm": gemm, "c": stage_c, "x": stage_x, "y": stage_y, "f": stage_f,
        "fx": stage_fx, "fc": stage_fc, "docs": documents, "outer": outer,
        "zw": z_wait, "gw": g_wait,
    }
    act_copy.wait()
    for name, *at in SCHEDULE:
        steps[name](*at)
    for copy in started:
        copy.wait_send()


def body(activations, gradients, eigvec_in, eigvec_out, lengths):
    anywhere = pl.BlockSpec(memory_space=pltpu.HBM)
    dma = pltpu.SemaphoreType.DMA
    return pl.pallas_call(
        kernel,
        out_shape=jax.ShapeDtypeStruct((1024, 256), F32),
        in_specs=[anywhere] * 4 + [pl.BlockSpec(memory_space=pltpu.SMEM)],
        out_specs=pl.BlockSpec(memory_space=pltpu.VMEM),
        scratch_shapes=[
            pltpu.VMEM((768, 896), BF16),
            pltpu.VMEM((32, 8192), BF16),
            pltpu.VMEM((896, 1024), BF16),
            pltpu.VMEM((8192, 256), BF16),
            pltpu.VMEM((768, 256), BF16),
            pltpu.VMEM((768, 512), BF16),
            pltpu.VMEM((8, 768, 128), F32),
            pltpu.VMEM((8, 384, 128), F32),
            pltpu.VMEM((8, 192, 128), BF16),
            pltpu.VMEM((8, 192, 128), BF16),
            pltpu.VMEM((8, 192, 128), BF16),
            pltpu.VMEM((7, 192, 128), BF16),
            pltpu.VMEM((8, 768, 128), BF16),
            pltpu.VMEM((8, 128, 512), F32),
            dma((7,)),
            dma((28,)),
            dma((28,)),
            dma((14,)),
            dma((14,)),
            dma((19 * len(SIZES),)),
            dma((19 * len(SIZES),)),
        ],
        compiler_params=pltpu.CompilerParams(
            collective_id=0, has_side_effects=True, vmem_limit_bytes=60 * 1024 * 1024),
        cost_estimate=pl.CostEstimate(
            flops=2_300_000_000, bytes_accessed=8_000_000, transcendentals=0),
    )(activations, gradients, eigvec_in, eigvec_out, lengths)


def solution(mesh):
    in_specs = (P("eout", "ein"), P("eout", None), P("ein", "eout"), P(None, "ein"), P())
    out_specs = P("eout", "ein")
    return jax.shard_map(body, mesh=mesh, in_specs=in_specs, out_specs=out_specs, check_vma=False)
```

```python
import jax
import jax.numpy as jnp
from jax import lax
from jax.experimental import pallas as pl
from jax.experimental.pallas import tpu as pltpu
from jax.sharding import PartitionSpec as P

LEN = 384
MESH = pl.DeviceIdType.MESH
F32 = jnp.float32
BF16 = jnp.bfloat16

NZ = 12
NY = 8
SIZES = (192, 128, 128, 128, 192)
OFFS = tuple(sum(SIZES[:g]) for g in range(len(SIZES)))
SLOT = 64
HALF = 32
SCHEDULE = [
    ("z0",), ("wi",), ("grad1",), ("z", 0, 1), ("z", 2, 0), ("grad2",), ("z", 2, 1), ("mm", 1),
    ("zw", 1), ("mm", 0), ("c", 1), ("c", 0), ("z", 4, 0), ("x", 1), ("z", 4, 1), ("zw", 3),
    ("mm", 2), ("mm", 3), ("x", 0), ("c", 2), ("c", 3), ("y", 1), ("g", 0), ("zw", 6), ("zw", 5),
    ("mm", 4), ("x", 2), ("c", 4), ("x", 3), ("y", 0), ("g", 2), ("f", 1), ("x", 4), ("y", 3),
    ("gw", 3), ("f", 0), ("gw", 1), ("y", 2), ("y", 4), ("fx", 1), ("g", 4), ("fx", 0), ("f", 3),
    ("f", 2), ("fx", 3), ("gw", 5), ("f", 4), ("gw", 6), ("fx", 2), ("docs",), ("fc", 3), ("fc", 0),
    ("fc", 1), ("fc", 2), ("outer", 0), ("fx", 4), ("fc", 4), ("outer", 1),
]


def up(k):
    return 0 if k == 0 else 2 * k - 1


def down(k):
    return 2 * k if k < 6 else 11


def kernel(
    act_in, grad_in, wi_in, wo_in, lengths, out,
    act, grads, wi, wo, gall, gdoc, part, core_r, x_s, x_r, y_s, y_r, full, prod,
    local_sem, z_ss, z_rs, g_ss, g_rs, r_ss, r_rs,
):
    ein = lax.axis_index("ein")
    eout = lax.axis_index("eout")
    core = lax.rem(ein, 2)
    x_lo = lax.rem(lax.div(ein, 2), 2)
    y = lax.div(ein, 4)
    x_hi = lax.rem(eout, 2)
    z = lax.div(eout, 2)

    z_peer = {
        ("u", n): (ein, lax.rem(z + NZ - n, NZ) * 2 + x_hi) for n in (1, 2)
    } | {("d", n): (ein, lax.rem(z + n, NZ) * 2 + x_hi) for n in (1, 2)}
    hi_peer = (ein, z * 2 + 1 - x_hi)
    core_peer = (ein + 1 - 2 * core, eout)
    x_peer = (ein + 2 - 4 * x_lo, eout)
    y_of = [lax.rem(y + d, NY) for d in range(NY)]
    y_peer = [(y_of[d] * 4 + x_lo * 2 + core, eout) for d in range(NY)]

    act_copy = pltpu.make_async_copy(act_in, act.at[pl.ds(0, HALF)], local_sem.at[0])
    act_copy.start()
    grad_copy = pltpu.make_async_copy(grad_in, grads, local_sem.at[1])
    grad_copy.start()
    wo_copies = []
    for i in range(4):
        rows = pl.ds(i * 2048, 2048)
        wo_copies.append(pltpu.make_async_copy(wo_in.at[rows], wo.at[rows], local_sem.at[2 + i]))
        wo_copies[-1].start()
    wi_copy = pltpu.make_async_copy(wi_in, wi, local_sem.at[6])
    wi_copy.start()

    barrier = pltpu.get_barrier_semaphore()
    partners = [*z_peer.values(), hi_peer, core_peer, x_peer, *y_peer[1:]]
    for peer in partners:
        pl.semaphore_signal(barrier, inc=1, device_id=peer, device_id_type=MESH)
    pl.semaphore_wait(barrier, len(partners))

    started = []
    state = {}

    def send(src, dst, ss, rs, peer):
        copy = pltpu.make_async_remote_copy(
            src_ref=src, dst_ref=dst, send_sem=ss, recv_sem=rs,
            device_id=peer, device_id_type=MESH,
        )
        copy.start()
        started.append(copy)
        return copy

    z_in = {}

    def act_unit(slot, h):
        return act.at[pl.ds(slot * SLOT + h * HALF, HALF)]

    slot_of = {"u": up, "d": down}

    def z_send(way, k, h, n):
        if k + n == 6 and way != "ud"[h]:
            return
        i = (k + n) * 4 + h * 2 + "ud".index(way)
        to = 11 if k + n == 6 else slot_of[way](k + n)
        z_in[way, k + n, h] = send(
            act_unit(slot_of[way](k), h), act_unit(to, h), z_ss.at[i], z_rs.at[i], z_peer[way, n])

    def z_serve(k, h):
        if k == 0 and h == 1:
            state["hi_act"].wait_recv()
        for way in "ud":
            if k > 0:
                z_in[way, k, h].wait_recv()
            z_send(way, k, h, 2)
            if k > 0:
                z_send(way, k, h, 1)
        if k == 0:
            for way in "ud":
                z_send(way, k, h, 1)

    def z_wait(k):
        for h in range(2):
            for way in "ud":
                if (way, k, h) in z_in:
                    z_in[way, k, h].wait_recv()

    g_in = {}

    def g_rows(slot, h=None):
        if h is None:
            return gall.at[pl.ds(slot * SLOT, SLOT)]
        return gall.at[pl.ds(slot * SLOT + h * HALF, HALF)]

    def g_send(way, k, n):
        i = (k + n) * 2 + "ud".index(way)
        h = "ud".index(way) if k + n == 6 else None
        to = 11 if k + n == 6 else slot_of[way](k + n)
        g_in[way, k + n] = send(
            g_rows(slot_of[way](k), h), g_rows(to, h), g_ss.at[i], g_rs.at[i], z_peer[way, n])

    def g_serve(k):
        if k == 0:
            state["hi"].wait_recv()
        for way in "ud":
            if k > 0:
                g_in[way, k].wait_recv()
            g_send(way, k, 2)
            g_send(way, k, 1)

    def g_wait(k):
        for way in "ud":
            g_in[way, k].wait_recv()

    def grad_part(first, count, total):
        def step(i, acc):
            at = pl.multiple_of(i * 1024, 1024)
            return acc + jnp.dot(
                grads[:, pl.ds(at, 1024)], wo[pl.ds(at, 1024), :], preferred_element_type=F32)
        return lax.fori_loop(first, first + count, step, total)

    def grad_done(total):
        limit = jnp.where(z < NZ // 2, lengths[0], lengths[1])
        start = lax.rem(z, NZ // 2) * SLOT + x_hi * HALF
        position = start + lax.broadcasted_iota(jnp.int32, (HALF, 256), 0)
        gall[pl.ds(0, HALF), :] = jnp.where(position < limit, total, 0.0).astype(BF16)

    red = {}

    def off2(g):
        return OFFS[g] // 2

    def off4(g):
        return OFFS[g] // 4

    def quarter(g, c, x):
        n = SIZES[g] // 4
        return pl.ds(pl.multiple_of(OFFS[g] + (c * 2 + x) * n, 16), n)

    def sem(g, i):
        return r_ss.at[g * 19 + i], r_rs.at[g * 19 + i]

    def gemm(g):
        rows = pl.ds(OFFS[g], SIZES[g])

        def step(c, carry):
            cols = pl.ds(pl.multiple_of(c * 256, 256), 256)
            product = jnp.dot(act[rows, :], wi[:, cols], preferred_element_type=F32)
            part[2 * c, rows, :] = product[:, :128]
            part[2 * c + 1, rows, :] = product[:, 128:]
            return carry

        lax.fori_loop(0, 4, step, 0)
        n = SIZES[g] // 2
        theirs = pl.ds(pl.multiple_of(OFFS[g] + (1 - core) * n, 16), n)
        red["c", g] = send(part.at[:, theirs], core_r.at[:, pl.ds(off2(g), n)], *sem(g, 0), core_peer)

    def in_half(g, x):
        n = SIZES[g] // 4
        return pl.ds(pl.multiple_of(off2(g) + x * n, 16), n)

    def stage_c(g):
        red["c", g].wait_recv()
        n = SIZES[g] // 4
        mine, got = quarter(g, core, 1 - x_lo), in_half(g, 1 - x_lo)

        def step(b, carry):
            x_s[b, pl.ds(off4(g), n), :] = (part[b, mine, :] + core_r[b, got, :]).astype(BF16)
            return carry

        lax.fori_loop(0, NY, step, 0)
        rows = pl.ds(off4(g), n)
        red["x", g] = send(x_s.at[:, rows], x_r.at[:, rows], *sem(g, 1), x_peer)

    def chip_pair_sum(g, b):
        n = SIZES[g] // 4
        return (part[b, quarter(g, core, x_lo), :] + core_r[b, in_half(g, x_lo), :]
                + x_r[b, pl.ds(off4(g), n), :].astype(F32))

    def stage_x(g):
        red["x", g].wait_recv()
        n = SIZES[g] // 4
        rows = pl.ds(off4(g), n)

        def step(b, carry):
            y_s[b, rows, :] = chip_pair_sum(g, b).astype(BF16)
            return carry

        lax.fori_loop(0, NY, step, 0)
        for d in (4, 3, 5, 2, 6, 1, 7):
            red["y", g, d] = send(
                y_s.at[y_of[d], rows], y_r.at[d - 1, rows], *sem(g, 1 + d), y_peer[d])

    def stage_y(g):
        n = SIZES[g] // 4
        rows = pl.ds(off4(g), n)
        total = chip_pair_sum(g, y)
        for d in range(1, NY):
            red["y", g, d].wait_recv()
        for d in range(1, NY):
            total = total + y_r[d - 1, rows, :].astype(F32)
        mine = quarter(g, core, x_lo)
        full[y, mine, :] = total.astype(BF16)
        for d in (4, 3, 5, 2, 6, 1, 7):
            red["f", g, d] = send(
                full.at[y, mine], full.at[y, mine], *sem(g, 8 + d), y_peer[d])

    def stage_f(g):
        mine = quarter(g, core, x_lo)
        for d in range(1, NY):
            recv = pltpu.make_async_remote_copy(
                src_ref=full.at[y, mine], dst_ref=full.at[y_of[NY - d], mine],
                send_sem=sem(g, 8 + d)[0], recv_sem=sem(g, 8 + d)[1],
                device_id=y_peer[d], device_id_type=MESH)
            recv.wait_recv()
        red["fx", g] = send(full.at[:, mine], full.at[:, mine], *sem(g, 16), x_peer)
        red["fc", g] = send(full.at[:, mine], full.at[:, mine], *sem(g, 17), core_peer)

    def wait_at(g, i, c, x, peer):
        rows = quarter(g, c, x)
        pltpu.make_async_remote_copy(
            src_ref=full.at[:, rows], dst_ref=full.at[:, rows],
            send_sem=sem(g, i)[0], recv_sem=sem(g, i)[1],
            device_id=peer, device_id_type=MESH).wait_recv()

    def stage_fx(g):
        wait_at(g, 16, core, 1 - x_lo, x_peer)
        theirs = quarter(g, core, 1 - x_lo)
        red["fxc", g] = send(full.at[:, theirs], full.at[:, theirs], *sem(g, 18), core_peer)

    def stage_fc(g):
        wait_at(g, 17, 1 - core, x_lo, core_peer)
        wait_at(g, 18, 1 - core, 1 - x_lo, core_peer)

    def grad_first():
        grad_copy.wait()
        for copy in wo_copies[:2]:
            copy.wait()
        state["total"] = grad_part(0, 4, jnp.zeros((HALF, 256), F32))

    def grad_last():
        for copy in wo_copies[2:]:
            copy.wait()
        grad_done(grad_part(4, 4, state["total"]))
        state["hi"] = send(g_rows(0, 0), g_rows(0, 1), g_ss.at[0], g_rs.at[0], hi_peer)

    def documents():
        for slot in range(NZ):
            k = (slot + 1) // 2
            shift = k if slot % 2 else NZ - k
            doc = lax.div(lax.rem(z + shift, NZ), NZ // 2)
            rows = pl.ds(slot * SLOT, SLOT)
            values = gall[rows, :]
            zero = jnp.zeros_like(values)
            gdoc[rows, 0:256] = jnp.where(doc == 0, values, zero)
            gdoc[rows, 256:512] = jnp.where(doc == 1, values, zero)

    def outer(last):
        rows = pl.ds(OFFS[-1], SIZES[-1]) if last else pl.ds(0, OFFS[-1])
        if last:
            denominator = (lengths[0] + lengths[1]).astype(F32)

        def step(b, carry):
            both = lax.dot_general(
                full[b, rows, :], gdoc[rows, :], (((0,), (0,)), ((), ())),
                preferred_element_type=F32)
            if last:
                both = both + prod[b]
                squares = both[:, :256] * both[:, :256] + both[:, 256:] * both[:, 256:]
                out[pl.ds(pl.multiple_of(b * 128, 128), 128), :] = squares / denominator
            else:
                prod[b] = both
            return carry

        lax.fori_loop(0, NY, step, 0)

    def z_first():
        state["hi_act"] = send(act_unit(0, 0), act_unit(0, 1), z_ss.at[0], z_rs.at[0], hi_peer)
        z_serve(0, 0)

    steps = {
        "z0": z_first, "z": z_serve, "wi": wi_copy.wait, "g": g_serve, "grad1": grad_first,
        "grad2": grad_last, "mm": gemm, "c": stage_c, "x": stage_x, "y": stage_y, "f": stage_f,
        "fx": stage_fx, "fc": stage_fc, "docs": documents, "outer": outer,
        "zw": z_wait, "gw": g_wait,
    }
    act_copy.wait()
    for name, *at in SCHEDULE:
        steps[name](*at)
    for copy in started:
        copy.wait_send()


def body(activations, gradients, eigvec_in, eigvec_out, lengths):
    anywhere = pl.BlockSpec(memory_space=pltpu.HBM)
    dma = pltpu.SemaphoreType.DMA
    return pl.pallas_call(
        kernel,
        out_shape=pltpu.VMEM((1024, 256), F32),
        in_specs=[anywhere] * 4 + [pl.BlockSpec(memory_space=pltpu.SMEM)],
        out_specs=pl.BlockSpec(memory_space=pltpu.VMEM),
        scratch_shapes=[
            pltpu.VMEM((768, 896), BF16),
            pltpu.VMEM((32, 8192), BF16),
            pltpu.VMEM((896, 1024), BF16),
            pltpu.VMEM((8192, 256), BF16),
            pltpu.VMEM((768, 256), BF16),
            pltpu.VMEM((768, 512), BF16),
            pltpu.VMEM((8, 768, 128), F32),
            pltpu.VMEM((8, 384, 128), F32),
            pltpu.VMEM((8, 192, 128), BF16),
            pltpu.VMEM((8, 192, 128), BF16),
            pltpu.VMEM((8, 192, 128), BF16),
            pltpu.VMEM((7, 192, 128), BF16),
            pltpu.VMEM((8, 768, 128), BF16),
            pltpu.VMEM((8, 128, 512), F32),
            dma((7,)),
            dma((28,)),
            dma((28,)),
            dma((14,)),
            dma((14,)),
            dma((19 * len(SIZES),)),
            dma((19 * len(SIZES),)),
        ],
        compiler_params=pltpu.CompilerParams(
            collective_id=0, has_side_effects=True, vmem_limit_bytes=60 * 1024 * 1024),
        cost_estimate=pl.CostEstimate(
            flops=2_300_000_000, bytes_accessed=8_000_000, transcendentals=0),
    )(activations, gradients, eigvec_in, eigvec_out, lengths)


def solution(mesh):
    in_specs = (P("eout", "ein"), P("eout", None), P("ein", "eout"), P(None, "ein"), P())
    out_specs = P("eout", "ein")
    return jax.shard_map(body, mesh=mesh, in_specs=in_specs, out_specs=out_specs, check_vma=False)
```

```python
import jax
import jax.numpy as jnp
from jax import lax
from jax.experimental import pallas as pl
from jax.experimental.pallas import tpu as pltpu
from jax.sharding import PartitionSpec as P

LEN = 384
MESH = pl.DeviceIdType.MESH
F32 = jnp.float32
BF16 = jnp.bfloat16

NZ = 12
NY = 8
SLOT = 64
HALF = 32


def up(k):
    return 0 if k == 0 else 2 * k - 1


def down(k):
    return 2 * k if k < 6 else 11


GROUPS = (
    ((0, 0), (1, 0), (2, 0), (0, 1)),
    ((1, 1), (2, 1)),
    ((3, 0), (4, 0)),
    ((3, 1), (4, 1)),
    ((5, 0), (6, 0), (5, 1), (6, 1)),
)
ROW = {}
OFFS = []
for members in GROUPS:
    OFFS.append(len(ROW) * HALF)
    for k, h in members:
        for slot in sorted({up(k), down(k)}):
            ROW[slot, h] = len(ROW) * HALF
SIZES = [end - start for start, end in zip(OFFS, OFFS[1:] + [NZ * SLOT])]

SCHEDULE = [
    ("z0",), ("z", 0, 1), ("grad1",), ("z", 2, 0), ("wi",), ("grad2",), ("zw", 1, 0), ("mm", 0),
    ("c", 0), ("zw", 1, 1), ("z", 2, 1), ("mm", 1), ("z", 4, 0), ("c", 1), ("zw", 3, 0), ("mm", 2),
    ("x", 0), ("c", 2), ("z", 4, 1), ("x", 1), ("zw", 3, 1), ("mm", 3), ("x", 2), ("c", 3),
    ("y", 0), ("g", 0), ("zw", 6, 0), ("zw", 6, 1), ("zw", 5, 0), ("zw", 5, 1), ("mm", 4), ("y", 1),
    ("c", 4), ("y", 2), ("g", 2), ("x", 3), ("f", 1), ("x", 4), ("f", 2), ("gw", 3), ("f", 0),
    ("y", 3), ("g", 4), ("fx", 1), ("y", 4), ("f", 3), ("gw", 5), ("fx", 0), ("gw", 6), ("fx", 2),
    ("f", 4), ("gw", 1), ("docs",), ("fc", 0), ("fx", 3), ("fc", 2), ("fc", 3), ("fc", 1),
    ("outer", 0), ("fx", 4), ("fc", 4), ("outer", 1),
]


def kernel(
    act_in, grad_in, wi_in, wo_in, lengths, out,
    act, grads, wi, wo, gall, gdoc, part, core_r, x_s, x_r, y_s, y_r, full, prod,
    local_sem, z_ss, z_rs, g_ss, g_rs, r_ss, r_rs,
):
    ein = lax.axis_index("ein")
    eout = lax.axis_index("eout")
    core = lax.rem(ein, 2)
    x_lo = lax.rem(lax.div(ein, 2), 2)
    y = lax.div(ein, 4)
    x_hi = lax.rem(eout, 2)
    z = lax.div(eout, 2)

    z_peer = {
        ("u", n): (ein, lax.rem(z + NZ - n, NZ) * 2 + x_hi) for n in (1, 2)
    } | {("d", n): (ein, lax.rem(z + n, NZ) * 2 + x_hi) for n in (1, 2)}
    hi_peer = (ein, z * 2 + 1 - x_hi)
    core_peer = (ein + 1 - 2 * core, eout)
    x_peer = (ein + 2 - 4 * x_lo, eout)
    y_of = [lax.rem(y + d, NY) for d in range(NY)]
    y_peer = [(y_of[d] * 4 + x_lo * 2 + core, eout) for d in range(NY)]

    act_copy = pltpu.make_async_copy(act_in, act.at[pl.ds(0, HALF)], local_sem.at[0])
    act_copy.start()
    grad_copy = pltpu.make_async_copy(grad_in, grads, local_sem.at[1])
    grad_copy.start()
    wo_copies = []
    for i in range(4):
        rows = pl.ds(i * 2048, 2048)
        wo_copies.append(pltpu.make_async_copy(wo_in.at[rows], wo.at[rows], local_sem.at[2 + i]))
        wo_copies[-1].start()
    wi_copy = pltpu.make_async_copy(wi_in, wi, local_sem.at[6])
    wi_copy.start()

    barrier = pltpu.get_barrier_semaphore()
    partners = [*z_peer.values(), hi_peer, core_peer, x_peer, *y_peer[1:]]
    for peer in partners:
        pl.semaphore_signal(barrier, inc=1, device_id=peer, device_id_type=MESH)
    pl.semaphore_wait(barrier, len(partners))

    started = []
    state = {}

    def send(src, dst, ss, rs, peer):
        copy = pltpu.make_async_remote_copy(
            src_ref=src, dst_ref=dst, send_sem=ss, recv_sem=rs,
            device_id=peer, device_id_type=MESH,
        )
        copy.start()
        started.append(copy)
        return copy

    z_in = {}

    def act_unit(slot, h):
        return act.at[pl.ds(ROW[slot, h], HALF)]

    slot_of = {"u": up, "d": down}

    def z_send(way, k, h, n):
        if k + n == 6 and way != "ud"[h]:
            return
        i = (k + n) * 4 + h * 2 + "ud".index(way)
        to = 11 if k + n == 6 else slot_of[way](k + n)
        z_in[way, k + n, h] = send(
            act_unit(slot_of[way](k), h), act_unit(to, h), z_ss.at[i], z_rs.at[i], z_peer[way, n])

    def z_serve(k, h):
        if k == 0 and h == 1:
            state["hi_act"].wait_recv()
        for way in "ud":
            if k > 0:
                z_in[way, k, h].wait_recv()
                z_send(way, k, h, 2)
                z_send(way, k, h, 1)
            else:
                z_send(way, k, h, 2)
        if k == 0:
            for way in "ud":
                z_send(way, k, h, 1)

    def z_wait(k, h):
        for way in "ud":
            if (way, k, h) in z_in:
                z_in[way, k, h].wait_recv()

    g_in = {}

    def g_rows(slot, h=None):
        if h is None:
            return gall.at[pl.ds(slot * SLOT, SLOT)]
        return gall.at[pl.ds(slot * SLOT + h * HALF, HALF)]

    def g_send(way, k, n):
        i = (k + n) * 2 + "ud".index(way)
        h = "ud".index(way) if k + n == 6 else None
        to = 11 if k + n == 6 else slot_of[way](k + n)
        g_in[way, k + n] = send(
            g_rows(slot_of[way](k), h), g_rows(to, h), g_ss.at[i], g_rs.at[i], z_peer[way, n])

    def g_serve(k):
        if k == 0:
            state["hi"].wait_recv()
        for way in "ud":
            if k > 0:
                g_in[way, k].wait_recv()
            g_send(way, k, 2)
            g_send(way, k, 1)

    def g_wait(k):
        for way in "ud":
            g_in[way, k].wait_recv()

    def grad_part(first, count, total):
        def step(i, acc):
            at = pl.multiple_of(i * 1024, 1024)
            return acc + jnp.dot(
                grads[:, pl.ds(at, 1024)], wo[pl.ds(at, 1024), :], preferred_element_type=F32)
        return lax.fori_loop(first, first + count, step, total)

    def grad_done(total):
        limit = jnp.where(z < NZ // 2, lengths[0], lengths[1])
        start = lax.rem(z, NZ // 2) * SLOT + x_hi * HALF
        position = start + lax.broadcasted_iota(jnp.int32, (HALF, 256), 0)
        gall[pl.ds(0, HALF), :] = jnp.where(position < limit, total, 0.0).astype(BF16)

    red = {}

    def off2(g):
        return OFFS[g] // 2

    def off4(g):
        return OFFS[g] // 4

    def quarter(g, c, x):
        n = SIZES[g] // 4
        return pl.ds(pl.multiple_of(OFFS[g] + (c * 2 + x) * n, 16), n)

    def sem(g, i):
        return r_ss.at[g * 19 + i], r_rs.at[g * 19 + i]

    def gemm(g):
        rows = pl.ds(OFFS[g], SIZES[g])

        def step(c, carry):
            cols = pl.ds(pl.multiple_of(c * 256, 256), 256)
            product = jnp.dot(act[rows, :], wi[:, cols], preferred_element_type=F32)
            part[2 * c, rows, :] = product[:, :128]
            part[2 * c + 1, rows, :] = product[:, 128:]
            return carry

        lax.fori_loop(0, 4, step, 0)
        n = SIZES[g] // 2
        theirs = pl.ds(pl.multiple_of(OFFS[g] + (1 - core) * n, 16), n)
        red["c", g] = send(part.at[:, theirs], core_r.at[:, pl.ds(off2(g), n)], *sem(g, 0), core_peer)

    def in_half(g, x):
        n = SIZES[g] // 4
        return pl.ds(pl.multiple_of(off2(g) + x * n, 16), n)

    def stage_c(g):
        red["c", g].wait_recv()
        n = SIZES[g] // 4
        mine, got = quarter(g, core, 1 - x_lo), in_half(g, 1 - x_lo)

        def step(b, carry):
            x_s[b, pl.ds(off4(g), n), :] = (part[b, mine, :] + core_r[b, got, :]).astype(BF16)
            return carry

        lax.fori_loop(0, NY, step, 0)
        rows = pl.ds(off4(g), n)
        red["x", g] = send(x_s.at[:, rows], x_r.at[:, rows], *sem(g, 1), x_peer)

    def chip_pair_sum(g, b):
        n = SIZES[g] // 4
        return (part[b, quarter(g, core, x_lo), :] + core_r[b, in_half(g, x_lo), :]
                + x_r[b, pl.ds(off4(g), n), :].astype(F32))

    def stage_x(g):
        red["x", g].wait_recv()
        n = SIZES[g] // 4
        rows = pl.ds(off4(g), n)

        def step(b, carry):
            y_s[b, rows, :] = chip_pair_sum(g, b).astype(BF16)
            return carry

        lax.fori_loop(0, NY, step, 0)
        for d in (4, 3, 5, 2, 6, 1, 7):
            red["y", g, d] = send(
                y_s.at[y_of[d], rows], y_r.at[d - 1, rows], *sem(g, 1 + d), y_peer[d])

    def stage_y(g):
        n = SIZES[g] // 4
        rows = pl.ds(off4(g), n)
        total = chip_pair_sum(g, y)
        for d in range(1, NY):
            red["y", g, d].wait_recv()
        for d in range(1, NY):
            total = total + y_r[d - 1, rows, :].astype(F32)
        mine = quarter(g, core, x_lo)
        full[y, mine, :] = total.astype(BF16)
        for d in (4, 3, 5, 2, 6, 1, 7):
            red["f", g, d] = send(
                full.at[y, mine], full.at[y, mine], *sem(g, 8 + d), y_peer[d])

    def stage_f(g):
        mine = quarter(g, core, x_lo)
        for d in range(1, NY):
            recv = pltpu.make_async_remote_copy(
                src_ref=full.at[y, mine], dst_ref=full.at[y_of[NY - d], mine],
                send_sem=sem(g, 8 + d)[0], recv_sem=sem(g, 8 + d)[1],
                device_id=y_peer[d], device_id_type=MESH)
            recv.wait_recv()
        red["fx", g] = send(full.at[:, mine], full.at[:, mine], *sem(g, 16), x_peer)
        red["fc", g] = send(full.at[:, mine], full.at[:, mine], *sem(g, 17), core_peer)

    def wait_at(g, i, c, x, peer):
        rows = quarter(g, c, x)
        pltpu.make_async_remote_copy(
            src_ref=full.at[:, rows], dst_ref=full.at[:, rows],
            send_sem=sem(g, i)[0], recv_sem=sem(g, i)[1],
            device_id=peer, device_id_type=MESH).wait_recv()

    def stage_fx(g):
        wait_at(g, 16, core, 1 - x_lo, x_peer)
        theirs = quarter(g, core, 1 - x_lo)
        red["fxc", g] = send(full.at[:, theirs], full.at[:, theirs], *sem(g, 18), core_peer)

    def stage_fc(g):
        wait_at(g, 17, 1 - core, x_lo, core_peer)
        wait_at(g, 18, 1 - core, 1 - x_lo, core_peer)

    def grad_first():
        grad_copy.wait()
        for copy in wo_copies[:2]:
            copy.wait()
        state["total"] = grad_part(0, 4, jnp.zeros((HALF, 256), F32))

    def grad_last():
        for copy in wo_copies[2:]:
            copy.wait()
        grad_done(grad_part(4, 4, state["total"]))
        state["hi"] = send(g_rows(0, 0), g_rows(0, 1), g_ss.at[0], g_rs.at[0], hi_peer)

    def documents():
        for slot in range(NZ):
            k = (slot + 1) // 2
            shift = k if slot % 2 else NZ - k
            doc = lax.div(lax.rem(z + shift, NZ), NZ // 2)
            for h in range(2):
                rows = pl.ds(ROW[slot, h], HALF)
                values = gall[pl.ds(slot * SLOT + h * HALF, HALF), :]
                zero = jnp.zeros_like(values)
                gdoc[rows, 0:256] = jnp.where(doc == 0, values, zero)
                gdoc[rows, 256:512] = jnp.where(doc == 1, values, zero)

    def outer(last):
        rows = pl.ds(OFFS[-1], SIZES[-1]) if last else pl.ds(0, OFFS[-1])
        if last:
            scale = 1.0 / jnp.full((1, 256), lengths[0] + lengths[1], jnp.int32).astype(F32)

        def step(b, carry):
            both = lax.dot_general(
                full[b, rows, :], gdoc[rows, :], (((0,), (0,)), ((), ())),
                preferred_element_type=F32)
            if last:
                both = both + prod[b]
                squares = both[:, :256] * both[:, :256] + both[:, 256:] * both[:, 256:]
                out[pl.ds(pl.multiple_of(b * 128, 128), 128), :] = squares * scale
            else:
                prod[b] = both
            return carry

        lax.fori_loop(0, NY, step, 0)

    def z_first():
        state["hi_act"] = send(act_unit(0, 0), act_unit(0, 1), z_ss.at[0], z_rs.at[0], hi_peer)
        z_serve(0, 0)

    steps = {
        "z0": z_first, "z": z_serve, "wi": wi_copy.wait, "g": g_serve, "grad1": grad_first,
        "grad2": grad_last, "mm": gemm, "c": stage_c, "x": stage_x, "y": stage_y, "f": stage_f,
        "fx": stage_fx, "fc": stage_fc, "docs": documents, "outer": outer,
        "zw": z_wait, "gw": g_wait,
    }
    act_copy.wait()
    for name, *at in SCHEDULE:
        steps[name](*at)
    for copy in started:
        copy.wait_send()


def body(activations, gradients, eigvec_in, eigvec_out, lengths):
    anywhere = pl.BlockSpec(memory_space=pltpu.HBM)
    dma = pltpu.SemaphoreType.DMA
    return pl.pallas_call(
        kernel,
        out_shape=pltpu.VMEM((1024, 256), F32),
        in_specs=[anywhere] * 4 + [pl.BlockSpec(memory_space=pltpu.SMEM)],
        out_specs=pl.BlockSpec(memory_space=pltpu.VMEM),
        scratch_shapes=[
            pltpu.VMEM((768, 896), BF16),
            pltpu.VMEM((32, 8192), BF16),
            pltpu.VMEM((896, 1024), BF16),
            pltpu.VMEM((8192, 256), BF16),
            pltpu.VMEM((768, 256), BF16),
            pltpu.VMEM((768, 512), BF16),
            pltpu.VMEM((8, 768, 128), F32),
            pltpu.VMEM((8, 384, 128), F32),
            pltpu.VMEM((8, 192, 128), BF16),
            pltpu.VMEM((8, 192, 128), BF16),
            pltpu.VMEM((8, 192, 128), BF16),
            pltpu.VMEM((7, 192, 128), BF16),
            pltpu.VMEM((8, 768, 128), BF16),
            pltpu.VMEM((8, 128, 512), F32),
            dma((7,)),
            dma((28,)),
            dma((28,)),
            dma((14,)),
            dma((14,)),
            dma((19 * len(SIZES),)),
            dma((19 * len(SIZES),)),
        ],
        compiler_params=pltpu.CompilerParams(
            collective_id=0, has_side_effects=True, vmem_limit_bytes=60 * 1024 * 1024),
        cost_estimate=pl.CostEstimate(
            flops=2_300_000_000, bytes_accessed=8_000_000, transcendentals=0),
    )(activations, gradients, eigvec_in, eigvec_out, lengths)


def solution(mesh):
    in_specs = (P("eout", "ein"), P("eout", None), P("ein", "eout"), P(None, "ein"), P())
    out_specs = P("eout", "ein")
    return jax.shard_map(body, mesh=mesh, in_specs=in_specs, out_specs=out_specs, check_vma=False)
```

```python
import jax
import jax.numpy as jnp
from jax import lax
from jax.experimental import pallas as pl
from jax.experimental.pallas import tpu as pltpu
from jax.sharding import PartitionSpec as P

LEN = 384
MESH = pl.DeviceIdType.MESH
F32 = jnp.float32
BF16 = jnp.bfloat16

NZ = 12
NY = 8
SLOT = 64
HALF = 32


def up(k):
    return 0 if k == 0 else 2 * k - 1


def down(k):
    return 2 * k if k < 6 else 11


GROUPS = (
    ((0, 0), (1, 0), (2, 0), (0, 1)),
    ((1, 1), (2, 1)),
    ((3, 0), (4, 0)),
    ((3, 1), (4, 1)),
    ((5, 0), (6, 0), (5, 1), (6, 1)),
)
ROW = {}
OFFS = []
for members in GROUPS:
    OFFS.append(len(ROW) * HALF)
    for k, h in members:
        for slot in sorted({up(k), down(k)}):
            ROW[slot, h] = len(ROW) * HALF
SIZES = [end - start for start, end in zip(OFFS, OFFS[1:] + [NZ * SLOT])]

SCHEDULE = [
    ("z0",), ("z", 0, 1), ("grad1",), ("z", 2, 0), ("wi",), ("grad2",), ("zw", 1, 0), ("mm", 0),
    ("c", 0), ("zw", 1, 1), ("z", 2, 1), ("mm", 1), ("z", 4, 0), ("c", 1), ("zw", 3, 0), ("mm", 2),
    ("x", 0), ("c", 2), ("z", 4, 1), ("x", 1), ("zw", 3, 1), ("mm", 3), ("x", 2), ("c", 3),
    ("y", 0), ("g", 0), ("zw", 6, 0), ("zw", 6, 1), ("zw", 5, 0), ("zw", 5, 1), ("mm", 4), ("y", 1),
    ("c", 4), ("y", 2), ("g", 2), ("x", 3), ("f", 1), ("x", 4), ("f", 2), ("gw", 3), ("f", 0),
    ("y", 3), ("g", 4), ("fx", 1), ("y", 4), ("f", 3), ("gw", 5), ("fx", 0), ("gw", 6), ("fx", 2),
    ("f", 4), ("gw", 1), ("docs",), ("fc", 0), ("fx", 3), ("fc", 2), ("fc", 3), ("fc", 1),
    ("outer", 0), ("fx", 4), ("fc", 4), ("outer", 1),
]


def kernel(
    act_in, grad_in, wi_in, wo_in, lengths, out,
    act, grads, wi, wo, gall, gdoc, part, core_r, x_s, x_r, y_s, y_r, full, prod,
    local_sem, z_ss, z_rs, g_ss, g_rs, r_ss, r_rs,
):
    ein = lax.axis_index("ein")
    eout = lax.axis_index("eout")
    core = lax.rem(ein, 2)
    x_lo = lax.rem(lax.div(ein, 2), 2)
    y = lax.div(ein, 4)
    x_hi = lax.rem(eout, 2)
    z = lax.div(eout, 2)

    z_peer = {
        ("u", n): (ein, lax.rem(z + NZ - n, NZ) * 2 + x_hi) for n in (1, 2)
    } | {("d", n): (ein, lax.rem(z + n, NZ) * 2 + x_hi) for n in (1, 2)}
    hi_peer = (ein, z * 2 + 1 - x_hi)
    core_peer = (ein + 1 - 2 * core, eout)
    x_peer = (ein + 2 - 4 * x_lo, eout)
    y_of = [lax.rem(y + d, NY) for d in range(NY)]
    y_peer = [(y_of[d] * 4 + x_lo * 2 + core, eout) for d in range(NY)]

    barrier = pltpu.get_barrier_semaphore()
    partners = [*z_peer.values(), hi_peer, core_peer, x_peer, *y_peer[1:]]
    for peer in partners:
        pl.semaphore_signal(barrier, inc=1, device_id=peer, device_id_type=MESH)

    act_copy = pltpu.make_async_copy(act_in, act.at[pl.ds(0, HALF)], local_sem.at[0])
    act_copy.start()
    grad_copy = pltpu.make_async_copy(grad_in, grads, local_sem.at[1])
    grad_copy.start()
    wo_copies = []
    for i in range(4):
        rows = pl.ds(i * 2048, 2048)
        wo_copies.append(pltpu.make_async_copy(wo_in.at[rows], wo.at[rows], local_sem.at[2 + i]))
        wo_copies[-1].start()
    wi_copy = pltpu.make_async_copy(wi_in, wi, local_sem.at[6])
    wi_copy.start()

    pl.semaphore_wait(barrier, len(partners))

    started = []
    state = {}

    def send(src, dst, ss, rs, peer):
        copy = pltpu.make_async_remote_copy(
            src_ref=src, dst_ref=dst, send_sem=ss, recv_sem=rs,
            device_id=peer, device_id_type=MESH,
        )
        copy.start()
        started.append(copy)
        return copy

    z_in = {}

    def act_unit(slot, h):
        return act.at[pl.ds(ROW[slot, h], HALF)]

    slot_of = {"u": up, "d": down}

    def z_send(way, k, h, n):
        if k + n == 6 and way != "ud"[h]:
            return
        i = (k + n) * 4 + h * 2 + "ud".index(way)
        to = 11 if k + n == 6 else slot_of[way](k + n)
        own = act_in if k == 0 and h == 0 else act_unit(slot_of[way](k), h)
        z_in[way, k + n, h] = send(
            own, act_unit(to, h), z_ss.at[i], z_rs.at[i], z_peer[way, n])

    def z_serve(k, h):
        if k == 0 and h == 1:
            state["hi_act"].wait_recv()
        for way in "ud":
            if k > 0:
                z_in[way, k, h].wait_recv()
                z_send(way, k, h, 2)
                z_send(way, k, h, 1)
            else:
                z_send(way, k, h, 2)
        if k == 0:
            for way in "ud":
                z_send(way, k, h, 1)

    def z_wait(k, h):
        for way in "ud":
            if (way, k, h) in z_in:
                z_in[way, k, h].wait_recv()

    g_in = {}

    def g_rows(slot, h=None):
        if h is None:
            return gall.at[pl.ds(slot * SLOT, SLOT)]
        return gall.at[pl.ds(slot * SLOT + h * HALF, HALF)]

    def g_send(way, k, n):
        i = (k + n) * 2 + "ud".index(way)
        h = "ud".index(way) if k + n == 6 else None
        to = 11 if k + n == 6 else slot_of[way](k + n)
        g_in[way, k + n] = send(
            g_rows(slot_of[way](k), h), g_rows(to, h), g_ss.at[i], g_rs.at[i], z_peer[way, n])

    def g_serve(k):
        if k == 0:
            state["hi"].wait_recv()
        for way in "ud":
            if k > 0:
                g_in[way, k].wait_recv()
            g_send(way, k, 2)
            g_send(way, k, 1)

    def g_wait(k):
        for way in "ud":
            g_in[way, k].wait_recv()

    def grad_part(first, count, total):
        def step(i, acc):
            at = pl.multiple_of(i * 1024, 1024)
            return acc + jnp.dot(
                grads[:, pl.ds(at, 1024)], wo[pl.ds(at, 1024), :], preferred_element_type=F32)
        return lax.fori_loop(first, first + count, step, total)

    def grad_done(total):
        limit = jnp.where(z < NZ // 2, lengths[0], lengths[1])
        start = lax.rem(z, NZ // 2) * SLOT + x_hi * HALF
        position = start + lax.broadcasted_iota(jnp.int32, (HALF, 256), 0)
        gall[pl.ds(0, HALF), :] = jnp.where(position < limit, total, 0.0).astype(BF16)

    red = {}

    def off2(g):
        return OFFS[g] // 2

    def off4(g):
        return OFFS[g] // 4

    def quarter(g, c, x):
        n = SIZES[g] // 4
        return pl.ds(pl.multiple_of(OFFS[g] + (c * 2 + x) * n, 16), n)

    def sem(g, i):
        return r_ss.at[g * 19 + i], r_rs.at[g * 19 + i]

    def gemm(g):
        rows = pl.ds(OFFS[g], SIZES[g])

        def step(c, carry):
            cols = pl.ds(pl.multiple_of(c * 256, 256), 256)
            product = jnp.dot(act[rows, :], wi[:, cols], preferred_element_type=F32)
            part[2 * c, rows, :] = product[:, :128]
            part[2 * c + 1, rows, :] = product[:, 128:]
            return carry

        lax.fori_loop(0, 4, step, 0)
        n = SIZES[g] // 2
        theirs = pl.ds(pl.multiple_of(OFFS[g] + (1 - core) * n, 16), n)
        red["c", g] = send(part.at[:, theirs], core_r.at[:, pl.ds(off2(g), n)], *sem(g, 0), core_peer)

    def in_half(g, x):
        n = SIZES[g] // 4
        return pl.ds(pl.multiple_of(off2(g) + x * n, 16), n)

    def stage_c(g):
        red["c", g].wait_recv()
        n = SIZES[g] // 4
        mine, got = quarter(g, core, 1 - x_lo), in_half(g, 1 - x_lo)

        def step(b, carry):
            x_s[b, pl.ds(off4(g), n), :] = (part[b, mine, :] + core_r[b, got, :]).astype(BF16)
            return carry

        lax.fori_loop(0, NY, step, 0)
        rows = pl.ds(off4(g), n)
        red["x", g] = send(x_s.at[:, rows], x_r.at[:, rows], *sem(g, 1), x_peer)

    def chip_pair_sum(g, b):
        n = SIZES[g] // 4
        return (part[b, quarter(g, core, x_lo), :] + core_r[b, in_half(g, x_lo), :]
                + x_r[b, pl.ds(off4(g), n), :].astype(F32))

    def stage_x(g):
        red["x", g].wait_recv()
        n = SIZES[g] // 4
        rows = pl.ds(off4(g), n)

        def step(b, carry):
            y_s[b, rows, :] = chip_pair_sum(g, b).astype(BF16)
            return carry

        lax.fori_loop(0, NY, step, 0)
        for d in (4, 3, 5, 2, 6, 1, 7):
            red["y", g, d] = send(
                y_s.at[y_of[d], rows], y_r.at[d - 1, rows], *sem(g, 1 + d), y_peer[d])

    def stage_y(g):
        n = SIZES[g] // 4
        rows = pl.ds(off4(g), n)
        total = chip_pair_sum(g, y)
        for d in range(1, NY):
            red["y", g, d].wait_recv()
        for d in range(1, NY):
            total = total + y_r[d - 1, rows, :].astype(F32)
        mine = quarter(g, core, x_lo)
        full[y, mine, :] = total.astype(BF16)
        for d in (4, 3, 5, 2, 6, 1, 7):
            red["f", g, d] = send(
                full.at[y, mine], full.at[y, mine], *sem(g, 8 + d), y_peer[d])

    def stage_f(g):
        mine = quarter(g, core, x_lo)
        for d in range(1, NY):
            recv = pltpu.make_async_remote_copy(
                src_ref=full.at[y, mine], dst_ref=full.at[y_of[NY - d], mine],
                send_sem=sem(g, 8 + d)[0], recv_sem=sem(g, 8 + d)[1],
                device_id=y_peer[d], device_id_type=MESH)
            recv.wait_recv()
        red["fx", g] = send(full.at[:, mine], full.at[:, mine], *sem(g, 16), x_peer)
        red["fc", g] = send(full.at[:, mine], full.at[:, mine], *sem(g, 17), core_peer)

    def wait_at(g, i, c, x, peer):
        rows = quarter(g, c, x)
        pltpu.make_async_remote_copy(
            src_ref=full.at[:, rows], dst_ref=full.at[:, rows],
            send_sem=sem(g, i)[0], recv_sem=sem(g, i)[1],
            device_id=peer, device_id_type=MESH).wait_recv()

    def stage_fx(g):
        wait_at(g, 16, core, 1 - x_lo, x_peer)
        theirs = quarter(g, core, 1 - x_lo)
        red["fxc", g] = send(full.at[:, theirs], full.at[:, theirs], *sem(g, 18), core_peer)

    def stage_fc(g):
        wait_at(g, 17, 1 - core, x_lo, core_peer)
        wait_at(g, 18, 1 - core, 1 - x_lo, core_peer)

    def grad_first():
        grad_copy.wait()
        for copy in wo_copies[:2]:
            copy.wait()
        state["total"] = grad_part(0, 4, jnp.zeros((HALF, 256), F32))

    def grad_last():
        for copy in wo_copies[2:]:
            copy.wait()
        grad_done(grad_part(4, 4, state["total"]))
        state["hi"] = send(g_rows(0, 0), g_rows(0, 1), g_ss.at[0], g_rs.at[0], hi_peer)

    def documents():
        for slot in range(NZ):
            k = (slot + 1) // 2
            shift = k if slot % 2 else NZ - k
            doc = lax.div(lax.rem(z + shift, NZ), NZ // 2)
            for h in range(2):
                rows = pl.ds(ROW[slot, h], HALF)
                values = gall[pl.ds(slot * SLOT + h * HALF, HALF), :]
                zero = jnp.zeros_like(values)
                gdoc[rows, 0:256] = jnp.where(doc == 0, values, zero)
                gdoc[rows, 256:512] = jnp.where(doc == 1, values, zero)

    def outer(last):
        rows = pl.ds(OFFS[-1], SIZES[-1]) if last else pl.ds(0, OFFS[-1])
        if last:
            scale = 1.0 / jnp.full((1, 256), lengths[0] + lengths[1], jnp.int32).astype(F32)

        def step(b, carry):
            both = lax.dot_general(
                full[b, rows, :], gdoc[rows, :], (((0,), (0,)), ((), ())),
                preferred_element_type=F32)
            if last:
                both = both + prod[b]
                squares = both[:, :256] * both[:, :256] + both[:, 256:] * both[:, 256:]
                out[pl.ds(pl.multiple_of(b * 128, 128), 128), :] = squares * scale
            else:
                prod[b] = both
            return carry

        lax.fori_loop(0, NY, step, 0)

    def z_first():
        state["hi_act"] = send(act_in, act_unit(0, 1), z_ss.at[0], z_rs.at[0], hi_peer)
        z_serve(0, 0)

    steps = {
        "z0": z_first, "z": z_serve, "wi": wi_copy.wait, "g": g_serve, "grad1": grad_first,
        "grad2": grad_last, "mm": gemm, "c": stage_c, "x": stage_x, "y": stage_y, "f": stage_f,
        "fx": stage_fx, "fc": stage_fc, "docs": documents, "outer": outer,
        "zw": z_wait, "gw": g_wait,
    }
    for name, *at in SCHEDULE:
        if name == "wi":
            act_copy.wait()
        steps[name](*at)
    for copy in started:
        copy.wait_send()


def body(activations, gradients, eigvec_in, eigvec_out, lengths):
    anywhere = pl.BlockSpec(memory_space=pltpu.HBM)
    dma = pltpu.SemaphoreType.DMA
    return pl.pallas_call(
        kernel,
        out_shape=pltpu.VMEM((1024, 256), F32),
        in_specs=[anywhere] * 4 + [pl.BlockSpec(memory_space=pltpu.SMEM)],
        out_specs=pl.BlockSpec(memory_space=pltpu.VMEM),
        scratch_shapes=[
            pltpu.VMEM((768, 896), BF16),
            pltpu.VMEM((32, 8192), BF16),
            pltpu.VMEM((896, 1024), BF16),
            pltpu.VMEM((8192, 256), BF16),
            pltpu.VMEM((768, 256), BF16),
            pltpu.VMEM((768, 512), BF16),
            pltpu.VMEM((8, 768, 128), F32),
            pltpu.VMEM((8, 384, 128), F32),
            pltpu.VMEM((8, 192, 128), BF16),
            pltpu.VMEM((8, 192, 128), BF16),
            pltpu.VMEM((8, 192, 128), BF16),
            pltpu.VMEM((7, 192, 128), BF16),
            pltpu.VMEM((8, 768, 128), BF16),
            pltpu.VMEM((8, 128, 512), F32),
            dma((7,)),
            dma((28,)),
            dma((28,)),
            dma((14,)),
            dma((14,)),
            dma((19 * len(SIZES),)),
            dma((19 * len(SIZES),)),
        ],
        compiler_params=pltpu.CompilerParams(
            collective_id=0, has_side_effects=True, vmem_limit_bytes=60 * 1024 * 1024),
        cost_estimate=pl.CostEstimate(
            flops=2_300_000_000, bytes_accessed=8_000_000, transcendentals=0),
    )(activations, gradients, eigvec_in, eigvec_out, lengths)


def solution(mesh):
    in_specs = (P("eout", "ein"), P("eout", None), P("ein", "eout"), P(None, "ein"), P())
    out_specs = P("eout", "ein")
    return jax.shard_map(body, mesh=mesh, in_specs=in_specs, out_specs=out_specs, check_vma=False)
```
